32 devices in a mesh: rep: 4 (over z), dp: 8 (over y, x, core).
Axes of the slice: x: 2, y: 2, z: 4, core: 2. Of those that a mesh axis runs over, the one named last changes fastest.
Arguments:
- decoder_input: bfloat16 [32768, 512], P(('rep', 'dp')), may hold values from -20 to 20
- target_embedding: bfloat16 [32768, 512], P(('rep', 'dp')), may hold values from -20 to 20
- encoder_states: bfloat16 [32768, 512], P(('rep', 'dp')), may hold values from -20 to 20
- cotangent: float32 [32768, 512], P(('rep', 'dp')), may hold values from -6 to 6
- segments: int32 [32, 1024], P(('rep', 'dp')), may hold values from -1 to 50, as said below
- hamming: int32 [32, 51], P(('rep', 'dp')), may hold values from 0 to 63
- priority: int32 [32, 1024], P(('rep', 'dp')), may hold values from 0 to 1023
- attention_weight: float32 [8, 512, 512], P(None, 'dp')
- attention_first: float32 [8, 512, 512], P(None, 'dp')
- attention_second: float32 [8, 512, 512], P(None, 'dp'), as said below
- expand_weight: float32 [512, 2048], P('dp'), may hold values from -0.25 to 0.25
- expand_first: float32 [512, 2048], P('dp')
- expand_second: float32 [512, 2048], P('dp'), as said below
- contract_weight: float32 [2048, 512], P('dp'), may hold values from -0.125 to 0.125
- contract_first: float32 [2048, 512], P('dp')
- contract_second: float32 [2048, 512], P('dp'), as said below
- vector_weight: float32 [17, 512], P(None, 'dp')
- vector_first: float32 [17, 512], P(None, 'dp')
- vector_second: float32 [17, 512], P(None, 'dp'), as said below
Outputs:
- layer_output: bfloat16 [32768, 512], P(('rep', 'dp'))
- input_grad: float32 [32768, 512], P(('rep', 'dp'))
- encoder_grad: float32 [32768, 512], P(('rep', 'dp'))
- attention_grad: float32 [8, 512, 512], P(None, 'dp')
- attention_first_new: float32 [8, 512, 512], P(None, 'dp')
- attention_second_new: float32 [8, 512, 512], P(None, 'dp')
- attention_weight_new: float32 [8, 512, 512], P(None, 'dp')
- expand_grad: float32 [512, 2048], P('dp')
- expand_first_new: float32 [512, 2048], P('dp')
- expand_second_new: float32 [512, 2048], P('dp')
- expand_weight_new: float32 [512, 2048], P('dp')
- contract_grad: float32 [2048, 512], P('dp')
- contract_first_new: float32 [2048, 512], P('dp')
- contract_second_new: float32 [2048, 512], P('dp')
- contract_weight_new: float32 [2048, 512], P('dp')
- vector_grad: float32 [17, 512], P(None, 'dp')
- vector_first_new: float32 [17, 512], P(None, 'dp')
- vector_second_new: float32 [17, 512], P(None, 'dp')
- vector_weight_new: float32 [17, 512], P(None, 'dp')
- grad_norm: float32 [], replicated
The draws below stay inside these ranges and needn't reach their ends.
Inputs may be any that keep to these rules, and one draw needn't show every extreme that they name: `segments`: in each row, ids start at 0, never fall, each id is one run of positions, and padding (-1) stands only at the row's end. `attention_second`: Positive. `expand_second`: Positive. `contract_second`: Positive. `vector_second`: Positive.
All inputs are finite; a program needn't handle non-finite values.
Results may differ from the reference program's by a relative error of at most 0.023.
The reference program's roundings to bfloat16 on the way count: a program that leaves them out, or rounds other values in their place, can miss the bound.
Values may be sent and summed in bfloat16 or wider, within the bound.
A program may use at most 256 MiB of HBM per device.

```python
import math
import jax
import jax.numpy as jnp
from jax import lax

D = 512
H = 8
HD = 64
FF = 2048
ROW_LEN = 1024
STEP = 10
SLOTS = 51
VECS = 17
ROWS = 32
TOKENS = 32768


def feature_ramp(top):
    return 1.0 + (top - 1.0) * lax.broadcasted_iota(jnp.float32, (1, D), 1) / (D - 1)


def draw_decoder_input(key, part):
    key = jax.random.fold_in(key, 1)
    return (feature_ramp(3.0) * jax.random.truncated_normal(key, -4.0, 4.0, (TOKENS, D), jnp.float32)).astype(jnp.bfloat16)


def draw_target_embedding(key, part):
    key = jax.random.fold_in(key, 2)
    return (feature_ramp(3.0) * jax.random.truncated_normal(key, -4.0, 4.0, (TOKENS, D), jnp.float32)).astype(jnp.bfloat16)


def draw_encoder_states(key, part):
    key = jax.random.fold_in(key, 3)
    return (feature_ramp(3.0) * jax.random.truncated_normal(key, -4.0, 4.0, (TOKENS, D), jnp.float32)).astype(jnp.bfloat16)


def draw_vector_weight(key, part):
    key = jax.random.fold_in(key, 4)
    gain_key, bias_key = jax.random.split(key)
    row_ids = lax.broadcasted_iota(jnp.int32, (VECS, D), 0)
    is_gain = (row_ids == 0) | (row_ids == 2) | (row_ids == 4)
    column = lax.broadcasted_iota(jnp.float32, (VECS, D), 1) / (D - 1)
    ramp = 1.0 + 2.0 * column
    biases = 0.3 * jax.random.truncated_normal(bias_key, -4.0, 4.0, (VECS, D), jnp.float32)
    gains = ramp * jax.random.uniform(gain_key, (VECS, D), jnp.float32, 0.8, 1.2)
    return jnp.where(is_gain, gains, biases)


def draw_attention_weight(key, part):
    key = jax.random.fold_in(key, 5)
    factors = jnp.array([0.5, 0.5, 1.0, 2.83, 0.5, 0.5, 1.0, 2.83], jnp.float32) / math.sqrt(D)
    base = jax.random.truncated_normal(key, -4.0, 4.0, (8, D, D), jnp.float32)
    return factors[:, None, None] * base


def grad_scale():
    return 1.0 / math.sqrt(8 * D * D + 2 * D * FF + VECS * D)


def first_moment(key, shape, scale):
    return 0.111 * scale * jax.random.truncated_normal(key, -4.0, 4.0, shape, jnp.float32)


def second_moment(key, shape, scale):
    return 0.001 * scale * scale * jax.random.uniform(key, shape, jnp.float32, 1.0, 4.0)


def draw_attention_first(key, part):
    key = jax.random.fold_in(key, 11)
    return first_moment(key, (8, D, D), grad_scale())


def draw_attention_second(key, part):
    key = jax.random.fold_in(key, 12)
    return second_moment(key, (8, D, D), grad_scale())


def draw_expand_first(key, part):
    key = jax.random.fold_in(key, 13)
    return first_moment(key, (D, FF), grad_scale())


def draw_expand_second(key, part):
    key = jax.random.fold_in(key, 14)
    return second_moment(key, (D, FF), grad_scale())


def draw_contract_first(key, part):
    key = jax.random.fold_in(key, 15)
    return first_moment(key, (FF, D), grad_scale())


def draw_contract_second(key, part):
    key = jax.random.fold_in(key, 16)
    return second_moment(key, (FF, D), grad_scale())


def draw_vector_first(key, part):
    key = jax.random.fold_in(key, 17)
    return first_moment(key, (VECS, D), grad_scale())


def draw_vector_second(key, part):
    key = jax.random.fold_in(key, 18)
    return second_moment(key, (VECS, D), grad_scale())


def draw_segments(key, part):
    key = jax.random.fold_in(key, 7)
    shortest = ROW_LEN // 50
    longest = ROW_LEN // 10
    piece_key, doc_key, flag_key, pad_key = jax.random.split(key, 4)
    pieces = jax.random.randint(piece_key, (ROWS, SLOTS), shortest, longest + 1)
    doc_length = jax.random.randint(doc_key, (ROWS,), ROW_LEN // 2, ROW_LEN - ROW_LEN // 8 + 1)
    has_doc = jax.random.randint(flag_key, (ROWS,), 0, 4) == 0
    slot_pos = lax.broadcasted_iota(jnp.int32, (ROWS, SLOTS), 1)
    pieces = jnp.where((slot_pos == 0) & has_doc[:, None], doc_length[:, None], pieces)
    row_zero = lax.broadcasted_iota(jnp.int32, (ROWS, SLOTS), 0) == 0
    pieces = jnp.where(row_zero, shortest, pieces)
    padding = jax.random.randint(pad_key, (ROWS,), 0, ROW_LEN // 16)
    padding = jnp.where(row_zero[:, 0], ROW_LEN - SLOTS * shortest, padding)
    ends = jnp.cumsum(pieces, axis=1)
    position = lax.broadcasted_iota(jnp.int32, (ROWS, ROW_LEN, 1), 1)
    seg_ids = jnp.sum((ends[:, None, :] <= position).astype(jnp.int32), axis=2)
    seg_ids = jnp.minimum(seg_ids, SLOTS - 1)
    content = ROW_LEN - padding
    return jnp.where(position[:, :, 0] < content[:, None], seg_ids, -1).astype(jnp.int32)


def place_ends(drawn, rng, low, largest):
    longest = drawn.shape.index(max(drawn.shape))
    spots = []
    for shift in (0, 1):
        where = [jax.random.randint(jax.random.fold_in(rng, axis), (), 0, length) for axis, length in enumerate(drawn.shape)]
        where[longest] = (where[longest] + shift) % drawn.shape[longest]
        spots.append(tuple(where))
    return drawn.at[spots[0]].set(low).at[spots[1]].set(largest)


def levels(stream_key, shape, cuts, least, top_value):
    factor_of, own = 1.0, jax.random.fold_in(stream_key, 6)
    for dim, shards_of in cuts:
        steps = jnp.exp(jax.random.uniform(jax.random.fold_in(own, dim), (shards_of,), jnp.float32, least / len(cuts), top_value / len(cuts)))
        factor_of = factor_of * jnp.repeat(steps, shape[dim] // shards_of).reshape([-1 if axis == dim else 1 for axis in range(len(shape))])
    return factor_of


def bell_draw(key, dims, deviation, most, cuts=(), held_as=jnp.bfloat16):
    values = deviation * jax.random.normal(key, dims, jnp.float32)
    if cuts:
        values = values * levels(key, dims, cuts, -0.22, 0.18)
    return jnp.clip(values, -most, most).astype(held_as)


def setup_inputs(seed: int = 0) -> dict:
    streams_of = jax.random.split(jax.random.key(seed), 20)
    return {
        "decoder_input": draw_decoder_input(jax.random.fold_in(streams_of[19], 71), 0),
        "target_embedding": draw_target_embedding(jax.random.fold_in(streams_of[19], 71), 0),
        "encoder_states": draw_encoder_states(jax.random.fold_in(streams_of[19], 71), 0),
        "cotangent": bell_draw(streams_of[3], (TOKENS, D), 1.0, 6.0, ((0, 32),), jnp.float32),
        "segments": draw_segments(jax.random.fold_in(streams_of[19], 71), 0),
        "hamming": place_ends(jax.random.randint(streams_of[5], (ROWS, SLOTS), 0, ROW_LEN // 16), jax.random.fold_in(streams_of[5], 1), 0, (ROW_LEN // 16) - 1).astype(jnp.int32),
        "priority": place_ends(jax.random.randint(streams_of[6], (ROWS, ROW_LEN), 0, ROW_LEN), jax.random.fold_in(streams_of[6], 1), 0, ROW_LEN - 1).astype(jnp.int32),
        "attention_weight": draw_attention_weight(jax.random.fold_in(streams_of[19], 71), 0),
        "attention_first": draw_attention_first(jax.random.fold_in(streams_of[19], 71), 0),
        "attention_second": draw_attention_second(jax.random.fold_in(streams_of[19], 71), 0),
        "expand_weight": bell_draw(streams_of[10], (D, FF), D ** -0.5, 0.25, ((0, 8),), jnp.float32),
        "expand_first": draw_expand_first(jax.random.fold_in(streams_of[19], 71), 0),
        "expand_second": draw_expand_second(jax.random.fold_in(streams_of[19], 71), 0),
        "contract_weight": bell_draw(streams_of[13], (FF, D), FF ** -0.5, 0.125, ((0, 8),), jnp.float32),
        "contract_first": draw_contract_first(jax.random.fold_in(streams_of[19], 71), 0),
        "contract_second": draw_contract_second(jax.random.fold_in(streams_of[19], 71), 0),
        "vector_weight": draw_vector_weight(jax.random.fold_in(streams_of[19], 71), 0),
        "vector_first": draw_vector_first(jax.random.fold_in(streams_of[19], 71), 0),
        "vector_second": draw_vector_second(jax.random.fold_in(streams_of[19], 71), 0),
    }


@jax.custom_vjp
def low(v):
    return lax.optimization_barrier(v.astype(jnp.bfloat16)).astype(jnp.float32)

@jax.custom_vjp
def low_back(v):
    return v

def low_keep(v):
    return (low(v), None)

def low_pass(kept, grad):
    return (grad,)

def back_keep(v):
    return (v, None)

def back_low(kept, grad):
    return (low(grad),)
low.defvjp(low_keep, low_pass)
low_back.defvjp(back_keep, back_low)
NORM_EPS = 1e-05
CLIP_NORM = 1.0
BETA_ONE = 0.9
BETA_TWO = 0.999
ADAM_EPS = 1e-08
WEIGHT_DECAY = 0.01
RATE_MATRIX = 0.03
RATE_VECTOR = 0.5
NEG_FILL = -1000000000.0
PRECISION_HIGH = lax.Precision.HIGHEST

def rounded_both(values):
    return low_back(low(values))

def product(left, right):
    return jnp.dot(left, right, precision=PRECISION_HIGH)

def layer_norm(values, gain, shift):
    center = lax.optimization_barrier(jnp.mean(values, axis=-1, keepdims=True))
    centred = values - center
    spread = lax.optimization_barrier(jnp.mean(centred * centred, axis=-1, keepdims=True))
    return centred * lax.rsqrt(spread + NORM_EPS) * gain + shift

def glance(segments, hamming, priority, slot_count):
    row_len = segments.shape[1]
    slot_ids = lax.broadcasted_iota(jnp.int32, (1, 1, slot_count), 2)
    member = (segments[:, :, None] == slot_ids).astype(jnp.int32)
    counts = lax.optimization_barrier(jnp.sum(member, axis=1, keepdims=True))
    seg_length = lax.optimization_barrier(jnp.sum(member * counts, axis=2))
    distance = lax.optimization_barrier(jnp.sum(member * hamming[:, None, :], axis=2))
    return 2 * priority * seg_length < distance * row_len

def attend(query_in, key_in, matrices, bias_query, bias_value, bias_out, segment_row):
    length = query_in.shape[0]
    scale = 1.0 / math.sqrt(HD)
    queries = rounded_both(product(query_in, matrices[0]) + bias_query).reshape(length, H, HD)
    key_rows = rounded_both(product(key_in, matrices[1])).reshape(length, H, HD)
    value_rows = rounded_both(product(key_in, matrices[2]) + bias_value).reshape(length, H, HD)
    scores = low_back(jnp.einsum('qhd,khd->hqk', queries, key_rows, precision=PRECISION_HIGH) * scale)
    same = segment_row[:, None] == segment_row[None, :]
    scores = jnp.where(same[None, :, :], scores, NEG_FILL)
    highest = lax.optimization_barrier(jnp.max(scores, axis=2, keepdims=True))
    raised = jnp.exp(scores - highest)
    shares = low(raised / lax.optimization_barrier(jnp.sum(raised, axis=2, keepdims=True)))
    mixed = jnp.einsum('hqk,khd->qhd', shares, value_rows, precision=PRECISION_HIGH)
    mixed = rounded_both(mixed.reshape(length, H * HD))
    return low_back(product(mixed, matrices[3]) + bias_out)

def adamw_update(grad, weight, first, second, factor, rate):
    clipped = grad * factor
    first_new = BETA_ONE * first + (1.0 - BETA_ONE) * clipped
    second_new = BETA_TWO * second + (1.0 - BETA_TWO) * clipped * clipped
    first_hat = first_new / (1.0 - BETA_ONE ** STEP)
    second_hat = second_new / (1.0 - BETA_TWO ** STEP)
    weight_new = weight - rate * (first_hat / (jnp.sqrt(second_hat) + ADAM_EPS) + WEIGHT_DECAY * weight)
    return (clipped, first_new, second_new, weight_new)

def reference(decoder_input, target_embedding, encoder_states, cotangent, segments, hamming, priority, attention_weight, attention_first, attention_second, expand_weight, expand_first, expand_second, contract_weight, contract_first, contract_second, vector_weight, vector_first, vector_second):
    row_count = segments.shape[0]
    glanced = glance(segments, hamming, priority, SLOTS).reshape(-1)
    layer_input = jnp.where(glanced[:, None], target_embedding, decoder_input).astype(jnp.float32)
    encoder_float = encoder_states.astype(jnp.float32)
    valid_mask = (segments >= 0).reshape(-1).astype(jnp.float32)

    def forward(attention_all, expand_all, contract_all, vector_all, inputs, encoded):
        attention_low = low(attention_all)
        expand_low = low(expand_all)
        contract_low = low(contract_all)
        vectors = low(vector_all)
        hidden_bias = vectors[13:].reshape(FF)

        def one_row(packed):
            row_in, row_enc, row_seg = packed
            first_sum = row_in + attend(row_in, row_in, attention_low[0:4], vectors[6], vectors[7], vectors[8], row_seg)
            first_norm = layer_norm(first_sum, vectors[0], vectors[1])
            cross = attend(low(first_norm), row_enc, attention_low[4:8], vectors[9], vectors[10], vectors[11], row_seg)
            second_norm = layer_norm(first_norm + cross, vectors[2], vectors[3])
            expanded = low_back(product(low(second_norm), expand_low) + hidden_bias)
            activated = low(jax.nn.gelu(expanded))
            branch = low_back(product(activated, contract_low) + vectors[12])
            return layer_norm(second_norm + branch, vectors[4], vectors[5])
        outputs = lax.map(jax.checkpoint(one_row), (inputs.reshape(row_count, ROW_LEN, D), encoded.reshape(row_count, ROW_LEN, D), segments))
        return outputs.reshape(row_count * ROW_LEN, D)
    output, pull = jax.vjp(forward, attention_weight, expand_weight, contract_weight, vector_weight, layer_input, encoder_float)
    grads = pull(cotangent * valid_mask[:, None])
    attention_raw, expand_raw, contract_raw, vector_raw, input_grad, encoder_grad = grads
    total_square = jnp.sum(attention_raw * attention_raw) + jnp.sum(expand_raw * expand_raw) + jnp.sum(contract_raw * contract_raw) + jnp.sum(vector_raw * vector_raw)
    grad_norm = jnp.sqrt(total_square)
    factor = CLIP_NORM / jnp.maximum(grad_norm, CLIP_NORM)
    attention_out = adamw_update(attention_raw, attention_weight, attention_first, attention_second, factor, RATE_MATRIX)
    expand_out = adamw_update(expand_raw, expand_weight, expand_first, expand_second, factor, RATE_MATRIX)
    contract_out = adamw_update(contract_raw, contract_weight, contract_first, contract_second, factor, RATE_MATRIX)
    vector_out = adamw_update(vector_raw, vector_weight, vector_first, vector_second, factor, RATE_VECTOR)
    return (output.astype(jnp.bfloat16), input_grad, encoder_grad, attention_out[0], attention_out[1], attention_out[2], attention_out[3], expand_out[0], expand_out[1], expand_out[2], expand_out[3], contract_out[0], contract_out[1], contract_out[2], contract_out[3], vector_out[0], vector_out[1], vector_out[2], vector_out[3], grad_norm)
```

```python
import functools
import math

import jax
import jax.numpy as jnp
from jax import lax
from jax.experimental import pallas as pl
from jax.experimental.pallas import tpu as pltpu
from jax.sharding import PartitionSpec as P

H = 8
STEP = 10
NORM_EPS = 1e-05
CLIP_NORM = 1.0
BETA_ONE = 0.9
BETA_TWO = 0.999
ADAM_EPS = 1e-08
WEIGHT_DECAY = 0.01
RATE_MATRIX = 0.03
RATE_VECTOR = 0.5
NEG_FILL = -1000000000.0
GELU_C = math.sqrt(2.0 / math.pi)
GELU_A = 0.044715
LOG2_E = math.log2(math.e)
NEG_TWO = NEG_FILL * LOG2_E
F32 = jnp.float32
LOW = jnp.bfloat16
MIB = 1 << 20
MESH = pl.DeviceIdType.MESH


def nn(left, right):
    return jnp.dot(left, right, preferred_element_type=F32)


def nt(left, right):
    return lax.dot_general(left, right, (((1,), (1,)), ((), ())), preferred_element_type=F32)


def tn(left, right):
    return lax.dot_general(left, right, (((0,), (0,)), ((), ())), preferred_element_type=F32)


def fold(values, op):
    rows = min(values.shape[0], 64 if values.shape[1] <= 256 else 32)
    total = values[0:rows]
    for i in range(1, values.shape[0] // rows):
        total = op(total, values[i * rows : (i + 1) * rows])
    while rows > 8:
        rows //= 2
        total = op(total[0:rows], total[rows : 2 * rows])
    return total


def colmax(values):
    return jnp.max(fold(values, jnp.maximum), axis=0, keepdims=True)


def colsum(values):
    return jnp.sum(fold(values.astype(F32), jnp.add), axis=0, keepdims=True)


def wide(column, width):
    return jnp.concatenate([column] * (width // 128), axis=1)


def normed(values):
    centred = values - jnp.mean(values, axis=-1, keepdims=True)
    rs = lax.rsqrt(jnp.mean(centred * centred, axis=-1, keepdims=True) + NORM_EPS)
    return centred * rs, rs


def norm_back(grad, xh, rs):
    first = jnp.mean(grad, axis=-1, keepdims=True)
    second = jnp.mean(grad * xh, axis=-1, keepdims=True)
    return rs * (grad - first - xh * second)


def step_kernel(
    nd, nr,
    seg, ham, pri, vec_w, dec, tgt, enc, cot, aw_h, ew_h, cw_h,
    out_h, ig_h, eg_h, ga_h, ge_h, gc_h, gvec, norm,
    wself, watt, w1, w2, x, e, qs, ks, vs, os, qc, kcr, vc, oc, xh1, rs1, h1, h2, z, du, df, dr, da, tb, tt,
    gcol, scol, lt, lterms, dterms, vec, vacc, gp, acc_k, acc_v, hamp,
    g1, g2, gcr, gse, gvo, gwo, gve, r1p, r2p, rzp, r1o, r2o, rzo, r1v, r2v, rzv, rze, rzc, zs, zv,
    vslots, nall,
    sems, gather_sems, reduce_sems, direct_sems, norm_sems, ready,
):
    tokens, width = x.shape
    hidden = du.shape[1]
    pairs = width // 128
    bt = 256
    blocks = tokens // bt
    wide_bt = min(512, tokens)
    wide_blocks = tokens // wide_bt
    slots = ham.shape[1]
    spots = nd // 2
    r = width // nd
    me = lax.axis_index("dp")
    rep = lax.axis_index("rep")
    spot, core = me // 2, me % 2

    def core_peer():
        return {"dp": me + 1 - 2 * core}

    def spot_at(o):
        return (spot + o) % spots

    def plane_peer(o):
        return {"dp": 2 * spot_at(o) + core}

    half = nr // 2
    low_side = rep < half
    to_centre = jnp.where(low_side, half - 1 - rep, rep - half)
    is_centre = to_centre == 0
    is_end = to_centre == half - 1
    not_centre = to_centre > 0
    not_end = to_centre < half - 1
    inward = {"rep": jnp.where(low_side, rep + 1, rep - 1)}
    outward = {"rep": jnp.where(low_side, rep - 1, rep + 1)}
    dp_peers = [{"dp": (me + o) % nd} for o in range(1, nd)]

    rep_peers = [{"rep": (rep + o) % nr} for o in range(1, nr)]

    def signal_all(sem):
        for peer in dp_peers + rep_peers:
            pl.semaphore_signal(sem, inc=1, device_id=peer, device_id_type=MESH)

    def wait_all(sem):
        pl.semaphore_wait(sem, len(dp_peers + rep_peers))

    def remote(src, dst, send, recv, peer):
        return pltpu.make_async_remote_copy(
            src_ref=src, dst_ref=dst, send_sem=send, recv_sem=recv, device_id=peer, device_id_type=MESH
        )

    def wait_bytes(ref, sem):
        pltpu.make_async_copy(ref, ref, sem).wait()

    def copy(i, src, dst):
        return pltpu.make_async_copy(src, dst, sems.at[i])

    proj_s, proj_c = (qs, ks, vs, os), (qc, kcr, vc, oc)
    third = 3 * 128
    load_att = copy(4, aw_h, xh1.at[pl.ds(0, 8 * r), :])
    chunks = hidden // width
    load_exp = [
        copy(8 + j, ew_h.at[:, pl.ds(j * width, width)], xh1.at[pl.ds((12 + j) * r, r), :])
        for j in range(chunks)
    ]
    load_con = copy(6, cw_h, xh1.at[pl.ds(8 * r, 4 * r), :])
    loads = [copy(0, dec, x), copy(1, tgt, tb), copy(2, enc, e), copy(3, cot, dr)]
    for c in [load_att] + loads[:2] + load_exp + [load_con] + loads[2:]:
        c.start()

    barrier = pltpu.get_barrier_semaphore()
    signal_all(barrier)

    def rows_of(i, size=bt):
        return pl.ds(pl.multiple_of(i * size, size), size)

    def loop(count, body):
        def wrapped(i, carry):
            body(i)
            return carry
        lax.fori_loop(0, count, wrapped, 0)

    def third_of(p):
        return pl.ds(pl.multiple_of(p * third, 128), third)

    def side(buf_width, k):
        part = buf_width // 2
        return pl.ds(pl.multiple_of(k * part, 128), part)

    groups = [
        (lambda q, b, p: vslots.at[q, b]),
        (lambda q, b, p: watt.at[pl.ds(0, 2), q, b]),
        (lambda q, b, p: watt.at[pl.ds(2, 3), q, b]),
        (lambda q, b, p: w1.at[q, b]),
        (lambda q, b, p: w2.at[q, b]),
        (lambda q, b, p: wself.at[q, b, :, third_of(p)]),
    ]
    halves = [
        None,
        (lambda q, b, k: watt.at[pl.ds(0, 2), q, b, :, side(width, k)]),
        (lambda q, b, k: watt.at[pl.ds(2, 3), q, b, :, side(width, k)]),
        (lambda q, b, k: w1.at[q, b, :, side(hidden, k)]),
        (lambda q, b, k: w2.at[q, b, :, side(width, k)]),
    ]
    my_half = rep % 2
    twin = {"rep": rep + 1 - 2 * (rep % 2)}
    qkv = 5
    every = pl.ds(0, spots)
    others = pl.ds(0, spots - 1)

    def plane_part(i, q, b, p):
        return groups[i](q, b, p) if i in (0, qkv) else halves[i](q, b, my_half)

    def send_group(i, p=0):
        own = plane_part(i, spot, core, p)
        for o in range(1, spots):
            remote(own, own, gather_sems.at[0, i + p], gather_sems.at[1, i + p], plane_peer(o)).start()

    def pass_group(i):
        wait_bytes(halves[i](others, 0, 0), gather_sems.at[1, i])
        for o in range(1, spots):
            got = halves[i](spot_at(o), core, my_half)
            remote(got, got, gather_sems.at[4, i], gather_sems.at[5, i], twin).start()

    def forward_group(i, p=0):
        if i in (0, qkv):
            wait_bytes(groups[i](others, 0, p), gather_sems.at[1, i + p])
        else:
            wait_bytes(halves[i](others, 0, 0), gather_sems.at[5, i])
        mine = groups[i](every, core, p)
        remote(mine, mine, gather_sems.at[2, i + p], gather_sems.at[3, i + p], core_peer()).start()

    def use_group(i, p=0):
        wait_bytes(groups[i](every, 0, p), gather_sems.at[3, i + p])

    def finish_group(i, p=0):
        wait_bytes(groups[i](every, 0, p), gather_sems.at[2, i + p])
        if i in (0, qkv):
            wait_bytes(groups[i](others, 0, p), gather_sems.at[0, i + p])
        else:
            wait_bytes(halves[i](others, 0, 0), gather_sems.at[0, i])
            wait_bytes(halves[i](others, 0, 0), gather_sems.at[4, i])

    own_width = vec_w.shape[1]
    vslots[spot, core] = jnp.zeros(vslots.shape[2:], LOW)
    vec[...] = jnp.zeros_like(vec)
    vec[0 : vec_w.shape[0], 0:own_width] = vec_w[...]
    vslots[spot, core] = vec[:, 0:128].astype(LOW)

    def cast_att(first, count):
        for k in range(first, first + count):
            watt[k - 3, spot, core] = xh1[k * r : (k + 1) * r, :].astype(LOW)

    load_att.wait()
    for p in range(pairs):
        for k in range(3):
            at = p * third + k * 128
            wself[spot, core, :, at : at + 128] = xh1[
                k * r : (k + 1) * r, p * 128 : (p + 1) * 128
            ].astype(LOW)
    wait_all(barrier)
    send_group(0)
    for p in range(pairs):
        send_group(qkv, p)
    cast_att(3, 2)
    send_group(1)
    cast_att(5, 3)
    send_group(2)
    for j in range(chunks):
        load_exp[j].wait()
        w1[spot, core, :, j * width : (j + 1) * width] = xh1[
            (12 + j) * r : (13 + j) * r, :
        ].astype(LOW)
    send_group(3)
    load_con.wait()
    w2[spot, core] = xh1[8 * r : 12 * r, :].astype(LOW)
    send_group(4)

    vacc[...] = jnp.zeros_like(vacc)
    seg_row = seg[...].astype(F32)
    slot_pad = (slots + 63) // 64 * 64
    slot_ids = lax.broadcasted_iota(jnp.int32, (slot_pad, tokens), 0).astype(F32)
    member = jnp.where(slot_ids == seg_row, 1.0, 0.0)
    length = jnp.sum(member * jnp.sum(member, axis=1, keepdims=True), axis=0, keepdims=True)
    hamp[...] = jnp.zeros_like(hamp)
    hamp[0:1, 0:slots] = ham[...].astype(F32)
    distance = nn(hamp[:, 0:slot_pad].astype(LOW), member.astype(LOW))[0:1]
    glanced = jnp.where(
        2.0 * pri[...].astype(F32) * length < distance * float(tokens), 1.0, 0.0
    )
    gcol[...] = jnp.broadcast_to(glanced, (128, tokens)).T
    scol[...] = jnp.broadcast_to(seg_row, (128, tokens)).T

    lane = lax.broadcasted_iota(jnp.int32, (1, 128), 1)
    mask_f = (jnp.where(lane < 64, 1.0, 0.0), jnp.where(lane < 64, 0.0, 1.0))
    mask = (mask_f[0].astype(LOW), mask_f[1].astype(LOW))
    is_low = lane < 64

    def lanes_of(p):
        return pl.ds(pl.multiple_of(p * 128, 128), 128)

    for c in loads[:2]:
        c.wait()

    def choose(i):
        rows = rows_of(i)
        x[rows, :] = jnp.where(
            wide(gcol[rows, :], width) > 0.5, tb[rows, :].astype(F32), x[rows, :].astype(F32)
        ).astype(LOW)

    loop(blocks, choose)

    forward_group(0)
    forward_group(qkv, 0)
    use_group(0)
    vec_sum = jnp.zeros(vec.shape, F32)
    src_lane = lax.broadcasted_iota(jnp.int32, (128, width), 0)
    dst_lane = lax.broadcasted_iota(jnp.int32, (128, width), 1)
    for d in range(nd):
        pick = jnp.where(
            (dst_lane == src_lane + d * own_width) & (src_lane < own_width), 1.0, 0.0
        ).astype(LOW)
        vec_sum = vec_sum + nn(vslots[d // 2, d % 2], pick)
    vec[...] = vec_sum

    def att_w(k):
        return watt[k - 3].reshape(width, width)

    def exp_w(j):
        return w1[:, :, :, j * width : (j + 1) * width].reshape(width, width)

    per = spots * width // hidden

    def con_w(j):
        return w2[j * per : (j + 1) * per].reshape(width, width)

    def self_in(p):
        lanes = lanes_of(p)
        pair_w = wself[:, :, :, third_of(p)].reshape(width, third)
        bias_q, bias_v = vec[6:7, lanes], vec[7:8, lanes]

        def block(i):
            rows = rows_of(i, wide_bt)
            made = nn(x[rows, :], pair_w)
            proj_s[0][rows, lanes] = ((made[:, 0:128] + bias_q) * (0.125 * LOG2_E)).astype(LOW)
            proj_s[1][rows, lanes] = made[:, 128:256].astype(LOW)
            proj_s[2][rows, lanes] = (made[:, 256:384] + bias_v).astype(LOW)

        loop(wide_blocks, block)

    qb = 256

    term_id = lane % 4

    def term_lanes(p):
        return ((lane % 64) // 4 == p) & (term_id < 3)

    def minus_terms(values):
        first = values.astype(LOW).astype(F32)
        second = (values - first).astype(LOW).astype(F32)
        third_term = values - first - second
        return -jnp.where(term_id == 0, first, jnp.where(term_id == 1, second, third_term))

    lterms[...] = jnp.zeros_like(lterms)
    ones_rows = jnp.ones((16, tokens), LOW)
    upper_rows = lax.broadcasted_iota(jnp.int32, (128, qb), 0) >= 64

    def attend(proj, which, before, after):
        def pair(p):
            before(p)
            lanes = lanes_of(p)
            keys = proj[1][:, lanes]
            turned = proj[2][:, lanes].T
            sides = [jnp.concatenate([turned[k : k + 64], ones_rows], axis=0) for k in (0, 64)]
            units = [(b, head) for b in range(tokens // qb) for head in (0, 1)]

            def scores_of(unit):
                b, head = unit
                return nt(keys, proj[0][b * qb : (b + 1) * qb, lanes] * mask[head])

            ahead = scores_of(units[0])
            for k, (b, head) in enumerate(units):
                scores = ahead
                if k + 1 < len(units):
                    ahead = scores_of(units[k + 1])
                rows = pl.ds(b * qb, qb)
                if head == 0:
                    logs, mixes = [], []
                same = wide(scol[...], qb) == seg_row[:, b * qb : (b + 1) * qb]
                scores = jnp.where(same, scores, NEG_TWO)
                top = colmax(scores)
                mixed = nn(sides[head], jnp.exp2(scores - top).astype(LOW))
                total = mixed[64:65]
                mixes.append(mixed[0:64] * (1.0 / total))
                logs.append(top + jnp.log2(total))
                lt[which, 2 * p + head, :, rows] = NEG_TWO - logs[head]
                if head == 0:
                    continue
                proj[3][rows, lanes] = jnp.concatenate(mixes, axis=0).T.astype(LOW)
                spread = jnp.where(upper_rows, logs[0], logs[1]).T
                lterms[which, rows, :] = jnp.where(
                    term_lanes(p), minus_terms(spread), lterms[which, rows, :].astype(F32)
                ).astype(LOW)
            after(p)
        loop(pairs, pair)

    def self_before(p):
        use_group(qkv, p)
        self_in(p)

        @pl.when(p < pairs - 1)
        def _():
            forward_group(qkv, p + 1)

    def self_hook(p):
        @pl.when(p == 0)
        def _():
            pass_group(1)

        @pl.when(p == 1)
        def _():
            pass_group(2)

        @pl.when(p == pairs - 2)
        def _():
            forward_group(1)
            pass_group(3)

        @pl.when(p == pairs - 1)
        def _():
            forward_group(2)

    attend(proj_s, 0, self_before, self_hook)
    use_group(1)
    use_group(2)
    loads[2].wait()

    def first_norm(i):
        rows = rows_of(i)
        total = x[rows, :].astype(F32) + nn(proj_s[3][rows, :], att_w(3)) + vec[8:9, :]
        xh, rs = normed(total)
        xh1[rows, :] = xh
        rs1[rows, :] = rs
        low = (xh * vec[0:1, :] + vec[1:2, :]).astype(LOW)
        h1[rows, :] = low
        proj_c[0][rows, :] = ((nn(low, att_w(4)) + vec[9:10, :]) * (0.125 * LOG2_E)).astype(LOW)

        enc_low = e[rows, :]
        proj_c[1][rows, :] = nn(enc_low, att_w(5)).astype(LOW)
        proj_c[2][rows, :] = (nn(enc_low, att_w(6)) + vec[10:11, :]).astype(LOW)

    loop(blocks, first_norm)
    pass_group(4)

    def cross_hook(p):
        @pl.when(p == 1)
        def _():
            forward_group(3)

        @pl.when(p == pairs - 2)
        def _():
            forward_group(4)

    attend(proj_c, 1, lambda p: None, cross_hook)

    loads[3].wait()
    use_group(3)
    use_group(4)
    def add_row(k, value):
        vacc[k : k + 1, :] += value

    def feed_forward(i):
        rows = rows_of(i)
        valid = jnp.where(wide(scol[rows, :], width) >= 0.0, 1.0, 0.0)
        start = xh1[rows, :] * vec[0:1, :] + vec[1:2, :]
        xh2, rs2 = normed(start + nn(proj_c[3][rows, :], att_w(7)) + vec[11:12, :])
        second = xh2 * vec[2:3, :] + vec[3:4, :]
        low = second.astype(LOW)
        tt[:, rows] = low.T
        branch_sum = second + vec[12:13, :]
        for j in range(chunks):
            cols = pl.ds(j * width, width)
            u = nn(low, exp_w(j)) + vec[13 + j : 14 + j, :]
            square = u * u
            th = jnp.tanh(GELU_C * u * (1.0 + GELU_A * square))
            half = 0.5 * (1.0 + th)
            z[rows, cols] = (u * half).astype(LOW)
            gp[:, cols] = (
                half + u * half * (1.0 - th) * (GELU_C * (1.0 + 3.0 * GELU_A * square))
            ).astype(LOW)
        xh3, rs3 = normed(branch_sum + nn(z[rows, :], w2[...].reshape(hidden, width)))
        tb[rows, :] = (xh3 * vec[4:5, :] + vec[5:6, :]).astype(LOW)
        grad = dr[rows, :] * valid
        add_row(5, colsum(grad))
        add_row(4, colsum(grad * xh3))
        third = norm_back(grad * vec[4:5, :], xh3, rs3)
        branch = third.astype(LOW)
        df[rows, :] = branch
        add_row(12, colsum(branch))
        for j in range(chunks):
            cols = pl.ds(j * width, width)
            inner = (nt(branch, con_w(j)) * gp[:, cols]).astype(LOW)
            du[rows, cols] = inner
            add_row(13 + j, colsum(inner))
        grad = third + nt(du[rows, :], w1[...].reshape(width, hidden))
        add_row(3, colsum(grad))
        add_row(2, colsum(grad * xh2))
        grad = norm_back(grad * vec[2:3, :], xh2, rs2)
        dr[rows, :] = grad
        low = grad.astype(LOW)
        da[rows, :] = low
        add_row(11, colsum(low))

    loop(blocks, feed_forward)
    out_copy = copy(0, tb, out_h)
    out_copy.start()
    for i in range(qkv):
        finish_group(i)
    for p in range(pairs):
        finish_group(qkv, p)
    signal_all(ready)

    def first_step(g):
        buf, one, _, _, sid = g
        remote(buf.at[:, 1 - core], one, reduce_sems.at[0, sid], reduce_sems.at[1, sid], core_peer()).start()

    def second_step(g):
        buf, one, two, _, sid = g
        wait_bytes(one, reduce_sems.at[1, sid])
        for q in range(spots):
            buf[q, core] = (buf[q, core].astype(F32) + one[q].astype(F32)).astype(LOW)
        for o in range(1, spots):
            remote(
                buf.at[spot_at(o), core], two.at[o - 1],
                reduce_sems.at[2, sid], reduce_sems.at[3, sid], plane_peer(o),
            ).start()

    def third_step(g):
        buf, _, two, (up, _), sid = g
        wait_bytes(two, reduce_sems.at[3, sid])
        total = buf[spot, core].astype(F32)
        for o in range(spots - 1):
            total = total + two[o].astype(F32)
        buf[spot, core] = total.astype(LOW)

        @pl.when(is_end & not_centre)
        def _():
            remote(buf.at[spot, core], up, reduce_sems.at[4, sid], reduce_sems.at[5, sid], inward).start()

    def fourth_step(g):
        buf, _, _, (up, down), sid = g
        own = buf.at[spot, core]

        @pl.when(not_end)
        def _():
            wait_bytes(up, reduce_sems.at[5, sid])
            buf[spot, core] = (own[...].astype(F32) + up[...].astype(F32)).astype(LOW)

        @pl.when(not_end & not_centre)
        def _():
            remote(own, up, reduce_sems.at[4, sid], reduce_sems.at[5, sid], inward).start()

        @pl.when(is_centre)
        def _():
            remote(own, down, reduce_sems.at[6, sid], reduce_sems.at[7, sid], inward).start()

    def fifth_step(g):
        buf, _, _, (up, down), sid = g

        @pl.when(is_centre)
        def _():
            wait_bytes(down, reduce_sems.at[7, sid])
            down[...] = (buf[spot, core].astype(F32) + down[...].astype(F32)).astype(LOW)

        @pl.when(is_centre & not_end)
        def _():
            remote(down, down, reduce_sems.at[8, sid], reduce_sems.at[9, sid], outward).start()

    def final_step(g):
        _, _, _, (up, down), sid = g

        @pl.when(not_centre)
        def _():
            wait_bytes(down, reduce_sems.at[9, sid])

        @pl.when(not_centre & not_end)
        def _():
            remote(down, down, reduce_sems.at[8, sid], reduce_sems.at[9, sid], outward).start()

        return down[...]

    def finish_sends(g):
        _, one, two, (up, down), sid = g
        wait_bytes(one, reduce_sems.at[0, sid])
        wait_bytes(two, reduce_sems.at[2, sid])

        @pl.when(not_centre)
        def _():
            wait_bytes(up, reduce_sems.at[4, sid])

        @pl.when(is_centre)
        def _():
            wait_bytes(down, reduce_sems.at[6, sid])

        @pl.when(not_end)
        def _():
            wait_bytes(down, reduce_sems.at[8, sid])

    def third_direct(g, every_rep, k):
        buf, _, two, _, sid = g
        wait_bytes(two, reduce_sems.at[3, sid])
        total = buf[spot, core].astype(F32)
        for o in range(spots - 1):
            total = total + two[o].astype(F32)
        every_rep[rep] = total.astype(LOW)
        for peer in rep_peers:
            own = every_rep.at[rep]
            remote(own, own, direct_sems.at[0, k], direct_sems.at[1, k], peer).start()

    def final_direct(every_rep, k):
        wait_bytes(every_rep.at[pl.ds(0, nr - 1)], direct_sems.at[1, k])
        total = every_rep[0].astype(F32)
        for q in range(1, nr):
            total = total + every_rep[q].astype(F32)
        return total

    def finish_direct(g, every_rep, k):
        _, one, two, _, sid = g
        wait_bytes(one, reduce_sems.at[0, sid])
        wait_bytes(two, reduce_sems.at[2, sid])
        wait_bytes(every_rep.at[pl.ds(0, nr - 1)], direct_sems.at[0, k])

    steps = (first_step, second_step, third_step, fourth_step, fifth_step)
    chunks_of = [pl.ds(j * width, width) for j in range(chunks)]
    rows_in = [pl.ds(j * r, r) for j in range(chunks)]
    grps = {}
    for j in range(chunks):
        c = chunks_of[j]
        grps["e", j] = (
            g1.at[:, :, :, c], w1.at[:, 0, :, c], w1.at[others, 1, :, c],
            (w1.at[spots - 1, 1, :, c], rze.at[:, c]), j,
        )
        c = rows_in[j]
        grps["c", j] = (
            g2.at[:, :, c], w2.at[:, 0, c], w2.at[others, 1, c],
            (w2.at[spots - 1, 1, c], rzc.at[c]), chunks + j,
        )
    for k, (name, buf) in enumerate((("vo", gvo), ("wo", gwo))):
        grps[name, 0] = (buf, r1o.at[k], r2o.at[k], (rzo.at[k, 0], rzo.at[k, 1]), 2 * chunks + k)
    grps["v", 0] = (gve, r1v, r2v, (rzv.at[0], rzv.at[1]), 2 * chunks + 2)
    for i in range(2 * pairs):
        name, buf = ("x", gcr) if i < pairs else ("s", gse)
        grps[name, i % pairs] = (
            buf.at[i % pairs], r1p.at[i], r2p.at[i], (rzp.at[i, 0], rzp.at[i, 1]), 2 * chunks + 3 + i,
        )

    def run_steps(text):
        for word in text:
            step, name = int(word[0]), word[1:]
            ids = range(chunks) if name in ("e", "c") else [0]
            if name[-1].isdigit():
                name, ids = name[:-1], [int(name[-1])]
            for k in ids:
                if (name, k) in grps:
                    steps[step - 1](grps[name, k])

    def run_table(table, p):
        for k, text in enumerate(table):
            if text:
                pl.when(p == k)(functools.partial(run_steps, text))

    def contract_grads(j):
        cols = pl.ds(pl.multiple_of(j * width, width), width)
        g2[pl.ds(j * per, per)] = tn(z[:, cols], df[...]).astype(LOW).reshape(per, 2, 4 * r, width)

    loop(chunks, contract_grads)
    wait_all(ready)
    run_steps(("1c",))

    def expand_grads(j):
        cols = pl.ds(pl.multiple_of(j * width, width), width)
        g1[:, :, :, cols] = nn(tt[...], du[:, cols]).astype(LOW).reshape(spots, 2, r, width)
        run_table([("1e0",), ("1e1", "2c0",), ("1e2", "2c1",), ("1e3", "2c2",)], j)

    loop(chunks, expand_grads)
    gvo[...] = tn(proj_c[3][...], da[...]).astype(LOW).reshape(spots, 2, r, width)
    run_steps(("1vo", "2c3", "2e0",))

    def part(buf, i):
        return buf.at[:, pl.ds(i * width, width)]

    do = part(z, 3)
    kt = du.at[pl.ds(0, width), pl.ds(0, tokens)]
    xt = du.at[pl.ds(0, width), pl.ds(tokens, tokens)]
    et = du.at[pl.ds(tokens // 2, width), pl.ds(0, tokens)]

    head_of = lax.broadcasted_iota(jnp.int32, (width, 128), 0) // 64
    place = lax.broadcasted_iota(jnp.int32, (width, 128), 1)
    sel = jnp.where(
        (head_of == (place % 64) // 4 * 2 + 1 - place // 64) & (place % 4 < 3), 1.0, 0.0
    ).astype(LOW)

    def before_attention(proj, base, rows, grad_low):
        mixed = nt(grad_low, att_w(base + 3)).astype(LOW)
        do[rows, :] = mixed
        prod = mixed.astype(F32) * proj[3][rows, :].astype(F32)
        high = prod.astype(LOW)
        rest = (prod - high.astype(F32)).astype(LOW)
        dterms[rows, :] = minus_terms(nn(high, sel) + nn(rest, sel)).astype(LOW)
        kt[:, rows] = proj[1][rows, :].T

    kb = kc = 256

    def attend_back(proj, which, places, hook, after):
        def pair(p):
            lanes = lanes_of(p)
            dq, dk, dv = places(p)
            acc_k[...] = jnp.zeros_like(acc_k)
            acc_v[...] = jnp.zeros_like(acc_v)
            ones = jnp.where(term_lanes(p), 1.0, 0.0).astype(LOW)
            ones_at = [ones * mask[1], ones * mask[0]]

            def stretch(i):
                units = [(b, c) for b in range(2) for c in range(tokens // kc)]
                made = {}

                def operands(b):
                    rows = rows_of(2 * i + b, kb)
                    queries = proj[0][rows, lanes]
                    grads = do[rows, lanes]
                    mq = [queries * mask[k] for k in (0, 1)]
                    mg = [grads * mask[k] for k in (0, 1)]
                    return (
                        seg[:, rows].astype(F32),
                        [mq[k] + lterms[which, rows, :] * mask[1 - k] for k in (0, 1)],
                        [mg[k] + dterms[rows, :] * mask[1 - k] for k in (0, 1)],
                        jnp.concatenate(mq, axis=0),
                        jnp.concatenate(mg, axis=0),
                        [lt[which, 2 * p + k, :, rows] for k in (0, 1)],
                    )

                def products(unit):
                    b, c = unit
                    if b not in made:
                        made[b] = operands(b)
                    _, with_logs, with_sums, _, _, _ = made[b]
                    part = slice(c * kc, (c + 1) * kc)
                    keys, values = proj[1][part, lanes], proj[2][part, lanes]
                    return [
                        (
                            nt(keys * mask[k] + ones_at[k], with_logs[k]),
                            nt(values * mask[k] + ones_at[k], with_sums[k]),
                        )
                        for k in (0, 1)
                    ]

                ahead = products(units[0])
                for n, (b, c) in enumerate(units):
                    now = ahead
                    if n + 1 < len(units):
                        ahead = products(units[n + 1])
                    ids, _, _, mq, mg, fills = made[b]
                    if c == 0:
                        parts = [jnp.zeros((64, kb), F32)] * 2
                    part = slice(c * kc, (c + 1) * kc)
                    same = wide(scol[part, :], kb) == ids
                    shares, score_grads = [], []
                    for head in (0, 1):
                        scores, inner = now[head]
                        share = jnp.exp2(jnp.where(same, scores, fills[head]))
                        shares.append(share.astype(LOW))
                        score_grads.append((share * inner).astype(LOW))
                        krows = pl.ds(pl.multiple_of(p * 128 + head * 64, 64), 64)
                        parts[head] = parts[head] + nn(kt[krows, part], score_grads[head])
                    acc_k[part, :] += nn(jnp.concatenate(score_grads, axis=1), mq)
                    acc_v[part, :] += nn(jnp.concatenate(shares, axis=1), mg)
                    if c + 1 == tokens // kc:
                        turned = (jnp.concatenate(parts, axis=0) * 0.125).T
                        dq[rows_of(2 * i + b, kb), :] = turned.astype(LOW)

                @pl.when(i == 0)
                def _():
                    hook(p)

            loop(tokens // kb // 2, stretch)
            dk[...] = (acc_k[...] * (1.0 / LOG2_E)).astype(LOW)
            dv[...] = acc_v[...].astype(LOW)
            after(p, lanes, dq, dk, dv)
        loop(pairs, pair)

    def bias_sums(first, lanes, dq, dv):
        vacc[first : first + 1, lanes] = colsum(dq[...])
        vacc[first + 1 : first + 2, lanes] = colsum(dv[...])

    def cross_places(p):
        lanes = lanes_of(p)
        return z.at[:, lanes], h2.at[:, lanes], df.at[:, lanes]

    def self_places(p):
        return tuple(z.at[:, pl.ds(pl.multiple_of(p * third + k * 128, 128), 128)] for k in range(3))

    def cross_ready(i):
        rows = rows_of(i, wide_bt)
        before_attention(proj_c, 4, rows, da[rows, :])
        xt[:, rows] = h1[rows, :].T
        et[:, rows] = e[rows, :].T

    loop(wide_blocks, cross_ready)
    run_steps(("2e1", "2e2", "2e3", "2vo",))

    def cross_after(p, lanes, dq, dk, dv):
        bias_sums(9, lanes, dq, dv)
        both = jnp.concatenate([dk[...], dv[...]], axis=1)
        grads = jnp.concatenate([nn(xt[...], dq[...]), nn(et[...], both)], axis=1)
        gcr[p] = grads.astype(LOW).reshape(spots, 2, r, third)
        run_table([("1x0", "3c0", "3c1",), ("1x1", "3e0", "3e1", "4c0", "4c1",), ("1x2", "3e2", "3e3", "3vo", "5c0", "5c1",), ("1x3", "3x1", "4e2", "4e3", "4vo",)], p)

    def cross_mid(p):
        run_table([(), ("2x0", "3c2", "3c3",), ("2x1", "4c2", "4c3",), ("2x2", "3x0", "4e0", "4e1", "5c2", "5c3",)], p)

    attend_back(proj_c, 1, cross_places, cross_mid, cross_after)
    out_copy.wait()

    def after_cross(i):
        rows = rows_of(i)
        grad = dr[rows, :] + nt(z[rows, 0:width], att_w(4))
        xh = xh1[rows, :]
        add_row(1, colsum(grad))
        add_row(0, colsum(grad * xh))
        grad = norm_back(grad * vec[0:1, :], xh, rs1[rows, :])
        dr[rows, :] = grad
        low = grad.astype(LOW)
        da[rows, :] = low
        add_row(8, colsum(low))
        before_attention(proj_s, 0, rows, low)
        xt[:, rows] = x[rows, :].T

    loop(blocks, after_cross)

    gwo[...] = tn(proj_s[3][...], da[...]).astype(LOW).reshape(spots, 2, r, width)
    run_steps(("1wo", "2x3", "3x2", "4x0", "5e",))

    def pack_vectors():
        low = vacc[...].astype(LOW)
        row_id = lax.broadcasted_iota(jnp.int32, (width, 128), 0)
        lane_id = lax.broadcasted_iota(jnp.int32, (width, 128), 1)
        for d in range(nd):
            pick = jnp.where(
                (row_id == lane_id + d * own_width) & (lane_id < own_width), 1.0, 0.0
            ).astype(LOW)
            gve[d // 2, d % 2] = nn(low, pick).astype(LOW)

    def put(first, total):
        h1[first * r : first * r + total.shape[0], :] = total

    def self_after(p, lanes, dq, dk, dv):
        bias_sums(6, lanes, dq, dv)
        gse[p] = nn(xt[...], z[:, third_of(p)]).astype(LOW).reshape(spots, 2, r, third)
        run_table([("1s0", "3x3", "4x2", "5x0",), ("1s1", "3s0", "4x3", "5x2",), ("1s2", "3s1", "5x3", "5wo",), ("1s3", "3s2", "5s1",)], p)

    def self_mid(p):
        run_table([("2wo", "4x1", "5vo",), ("2s0", "3wo", "5x1",), ("2s1", "4wo", "4s0",), ("2s2", "4s1", "5s0",)], p)

        @pl.when(p == pairs - 1)
        def _():
            for j in range(chunks):
                put(8 + j, final_step(grps["c", j]))
                put(12 + j, final_step(grps["e", j]))
            put(7, final_step(grps["vo", 0]))

    attend_back(proj_s, 0, self_places, self_mid, self_after)
    pack_vectors()
    run_steps(("1v",))

    def encoder_out(i):
        rows = pl.ds(i * wide_bt, wide_bt)
        e[rows, :] = (nt(h2[rows, :], att_w(5)) + nt(df[rows, :], att_w(6))).astype(LOW)
        copy(4 + i, e.at[rows, :], eg_h.at[rows, :]).start()

    def input_out(i):
        rows = pl.ds(i * wide_bt, wide_bt)
        da[rows, :] = (
            dr[rows, :] + nt(z[rows, 0 : 3 * width], wself[...].reshape(width, 3 * width))
        ).astype(LOW)

    last_pair = grps["s", pairs - 1]

    def put_pair(name, base, i, total=None):
        total = final_step(grps[name, i]) if total is None else total.astype(LOW)
        for k in range(3):
            h1[(base + k) * r : (base + k + 1) * r, i * 128 : (i + 1) * 128] = total[:, k * 128 : (k + 1) * 128]

    encoder_out(0)
    run_steps(("2v", "2s3", "4s2"))
    encoder_out(1)
    third_direct(last_pair, zs, 0)
    third_direct(grps["v", 0], zv, 1)
    run_steps(("5s2",))
    input_out(0)
    put(3, final_step(grps["wo", 0]))
    for i in range(pairs):
        put_pair("x", 4, i)
    input_out(1)
    ig_copy = copy(0, da, ig_h)
    ig_copy.start()
    for i in range(pairs - 1):
        put_pair("s", 0, i)
    gvec[...] = final_direct(zv, 1)
    put_pair("s", 0, pairs - 1, final_direct(zs, 0))

    stores = [
        copy(1, h1.at[pl.ds(0, 8 * r), :], ga_h),
        copy(3, h1.at[pl.ds(8 * r, 4 * r), :], gc_h),
    ] + [
        copy(8 + j, h1.at[pl.ds((12 + j) * r, r), :], ge_h.at[:, pl.ds(j * width, width)])
        for j in range(chunks)
    ]
    for c in stores:
        c.start()

    def square(values):
        return fold(values * values, jnp.add)

    squares = lax.fori_loop(
        0, 16, lambda i, had: had + square(h1[rows_of(i, r), :].astype(F32)), jnp.zeros((8, width), F32)
    )
    total = jnp.sum(jnp.sum(squares, axis=0, keepdims=True), axis=1, keepdims=True) + jnp.sum(
        jnp.sum(square(gvec[...]), axis=0, keepdims=True), axis=1, keepdims=True
    )
    nall[me] = jnp.broadcast_to(total, (8, 128))
    for peer in dp_peers:
        remote(nall.at[me], nall.at[me], norm_sems.at[0], norm_sems.at[1], peer).start()
    siblings = pl.ds(0, nd - 1)
    wait_bytes(nall.at[siblings], norm_sems.at[1])
    whole = nall[0]
    for q in range(1, nd):
        whole = whole + nall[q]
    norm[...] = jnp.sqrt(whole)
    wait_bytes(nall.at[siblings], norm_sems.at[0])

    finish_direct(grps.pop(("s", pairs - 1)), zs, 0)
    finish_direct(grps.pop(("v", 0)), zv, 1)
    for g in grps.values():
        finish_sends(g)
    for c in stores:
        c.wait()
    for i in range(wide_blocks):
        rows = pl.ds(i * wide_bt, wide_bt)
        copy(4 + i, e.at[rows, :], eg_h.at[rows, :]).wait()
    ig_copy.wait()


def run_step(nd, nr, seg, ham, pri, vec_w, dec, tgt, enc, cot, aw, ew, cw):
    tokens, width = dec.shape
    hidden = ew.shape[1]
    spots, r = nd // 2, width // nd
    count = 2 * (hidden // width) + 3 + 2 * (width // 128)
    pairs = width // 128
    any_spec = pl.BlockSpec(memory_space=pl.ANY)
    vmem = pl.BlockSpec(memory_space=pltpu.VMEM)
    low = functools.partial(pltpu.VMEM, dtype=LOW)
    full = functools.partial(pltpu.VMEM, dtype=F32)
    vr = (vec_w.shape[0] + 15) // 16 * 16
    dma = pltpu.SemaphoreType.DMA
    return pl.pallas_call(
        functools.partial(step_kernel, nd, nr),
        out_shape=(
            jax.ShapeDtypeStruct((tokens, width), LOW),
            jax.ShapeDtypeStruct((tokens, width), LOW),
            jax.ShapeDtypeStruct((tokens, width), LOW),
            jax.ShapeDtypeStruct((8 * r, width), LOW),
            jax.ShapeDtypeStruct((r, hidden), LOW),
            jax.ShapeDtypeStruct((4 * r, width), LOW),
            jax.ShapeDtypeStruct((vr, 128), F32),
            jax.ShapeDtypeStruct((8, 128), F32),
        ),
        in_specs=[vmem] * 4 + [any_spec] * 7,
        out_specs=[any_spec] * 6 + [vmem] * 2,
        scratch_shapes=[
            low((spots, 2, r, 3 * width)), low((5, spots, 2, r, width)), low((spots, 2, r, hidden)), low((spots, 2, 4 * r, width)),
            low((tokens, width)), low((tokens, width)),
            *[low((tokens, width)) for _ in range(8)],
            full((tokens, width)), full((tokens, 1)),
            low((tokens, width)), low((tokens, width)),
            low((tokens, hidden)), low((tokens, hidden)),
            low((tokens, width)), full((tokens, width)), low((tokens, width)),
            low((tokens, width)), low((width, tokens)),
            full((tokens, 128)), full((tokens, 128)),
            full((2, H, 1, tokens)), low((2, tokens, 128)), low((tokens, 128)),
            full((vr, width)), full((vr, width)),
            low((256, hidden)), full((tokens, 128)), full((tokens, 128)),
            full((8, 128)),
            low((spots, 2, r, hidden)), low((spots, 2, 4 * r, width)),
            low((pairs, spots, 2, r, 384)), low((pairs, spots, 2, r, 384)),
            low((spots, 2, r, width)), low((spots, 2, r, width)), low((spots, 2, vr, 128)),
            low((2 * pairs, spots, r, 384)), low((2 * pairs, spots - 1, r, 384)), low((2 * pairs, 2, r, 384)),
            low((2, spots, r, width)), low((2, spots - 1, r, width)), low((2, 2, r, width)),
            low((spots, vr, 128)), low((spots - 1, vr, 128)), low((2, vr, 128)),
            low((r, hidden)), low((4 * r, width)), low((nr, r, 384)), low((nr, vr, 128)),
            low((spots, 2, vr, 128)), full((nd, 8, 128)),
            dma((8 + hidden // width,)), dma((6, 5 + pairs)), dma((10, count)), dma((2, 2)), dma((2,)),
            pltpu.SemaphoreType.REGULAR,
        ],
        compiler_params=pltpu.CompilerParams(
            vmem_limit_bytes=64 * MIB - 64 * 1024, collective_id=0, has_side_effects=True
        ),
        cost_estimate=pl.CostEstimate(flops=41 * 10**9, bytes_accessed=30 * MIB, transcendentals=50 * 10**6),
        name="layer_step",
    )(seg, ham, pri, vec_w, dec, tgt, enc, cot, aw, ew, cw)


def adamw_kernel(*args):
    norm, args = args[0], args[1:]
    moved_in, raws, states = args[0:3], args[3:7], args[7:19]
    moved_out, outs, norm_out = args[19:22], args[22:38], args[38]
    bufs, sems = args[39:-1], args[-1]
    moved_a, moved_b, held, made = bufs[0:3], bufs[3:6], bufs[6:22], bufs[22:38]
    pending = []

    def copy(source, dest):
        c = pltpu.make_async_copy(source, dest, sems.at[len(pending)])
        pending.append(c)
        c.start()
        return c

    fetched = []
    for i in range(4):
        sources = (raws[i],) + states[3 * i : 3 * i + 3]
        fetched.append([copy(a, b) for a, b in zip(sources, held[4 * i : 4 * i + 4])])
    moves = [copy(a, b) for a, b in zip(moved_in, moved_a)]
    factor = CLIP_NORM / jnp.maximum(norm[0:1, 0:1], CLIP_NORM)
    norm_out[...] = norm[0:1, 0:1]
    stores = []
    for i in range(4):
        for c in fetched[i]:
            c.wait()
        raw, weight, first, second = (ref[...] for ref in held[4 * i : 4 * i + 4])
        rate = RATE_VECTOR if i == 3 else RATE_MATRIX
        clipped = raw[0 : weight.shape[0], 0 : weight.shape[1]].astype(F32) * factor
        first_new = BETA_ONE * first + (1.0 - BETA_ONE) * clipped
        second_new = BETA_TWO * second + (1.0 - BETA_TWO) * clipped * clipped
        first_hat = first_new / (1.0 - BETA_ONE**STEP)
        second_hat = second_new / (1.0 - BETA_TWO**STEP)
        weight_new = weight - rate * (
            first_hat / (jnp.sqrt(second_hat) + ADAM_EPS) + WEIGHT_DECAY * weight
        )
        for k, value in enumerate((clipped, first_new, second_new, weight_new)):
            made[4 * i + k][...] = value
            stores.append(copy(made[4 * i + k], outs[4 * i + k]))
    for k in range(3):
        moves[k].wait()
        if moved_a[k].dtype == moved_b[k].dtype:
            stores.append(copy(moved_a[k], moved_out[k]))
        else:
            moved_b[k][...] = moved_a[k][...].astype(moved_b[k].dtype)
            stores.append(copy(moved_b[k], moved_out[k]))
    for c in stores:
        c.wait()


def run_adamw(norm, moved, raws, states):
    any_spec = pl.BlockSpec(memory_space=pl.ANY)
    vmem = pl.BlockSpec(memory_space=pltpu.VMEM)
    flat = [a for state in states for a in state]
    moved_types = (LOW, F32, F32)
    made = [state[0].shape for state in states for _ in range(4)]
    held = [a for raw, state in zip(raws, states) for a in (raw,) + tuple(state)]
    scratch = [pltpu.VMEM(a.shape, a.dtype) for a in moved]
    scratch += [pltpu.VMEM(a.shape if d == F32 else (16, 128), d) for a, d in zip(moved, moved_types)]
    scratch += [pltpu.VMEM(a.shape, a.dtype) for a in held] + [pltpu.VMEM(m, F32) for m in made]
    outs = pl.pallas_call(
        adamw_kernel,
        in_specs=[vmem] + [any_spec] * 19,
        out_specs=[any_spec] * 19 + [vmem],
        out_shape=[jax.ShapeDtypeStruct(a.shape, d) for a, d in zip(moved, moved_types)]
        + [jax.ShapeDtypeStruct(m, F32) for m in made]
        + [jax.ShapeDtypeStruct((1, 1), F32)],
        scratch_shapes=scratch + [pltpu.SemaphoreType.DMA((38,))],
        compiler_params=pltpu.CompilerParams(vmem_limit_bytes=64 * MIB - 64 * 1024),
        cost_estimate=pl.CostEstimate(flops=10**7, bytes_accessed=21 * MIB, transcendentals=10**6),
        name="adamw",
    )(norm, *moved, *raws, *flat)
    return outs[3:19], outs[0:3], outs[19]


def per_device(
    nd,
    nr,
    decoder_input,
    target_embedding,
    encoder_states,
    cotangent,
    segments,
    hamming,
    priority,
    attention_weight,
    attention_first,
    attention_second,
    expand_weight,
    expand_first,
    expand_second,
    contract_weight,
    contract_first,
    contract_second,
    vector_weight,
    vector_first,
    vector_second,
):
    width = decoder_input.shape[1]
    attention = tuple(
        a.reshape(-1, width) for a in (attention_weight, attention_first, attention_second)
    )
    expand = (expand_weight, expand_first, expand_second)
    contract = (contract_weight, contract_first, contract_second)
    vector = (vector_weight, vector_first, vector_second)
    layer_output, input_grad, encoder_grad, ga, ge, gc, gv, norm = run_step(
        nd, nr, segments, hamming, priority, vector_weight, decoder_input, target_embedding,
        encoder_states, cotangent, attention[0], expand_weight, contract_weight,
    )
    outs, moved, whole_norm = run_adamw(
        norm, (layer_output, input_grad, encoder_grad), (ga, ge, gc, gv), (attention, expand, contract, vector)
    )
    attention_outs = tuple(a.reshape(attention_weight.shape) for a in outs[0:4])
    return tuple(moved) + attention_outs + tuple(outs[4:16]) + (whole_norm.reshape(()),)


def solution(mesh):
    rows = P(("rep", "dp"), None)
    owned = (P(None, "dp", None),) * 3 + (P("dp", None),) * 6 + (P(None, "dp"),) * 3
    made = (P(None, "dp", None),) * 4 + (P("dp", None),) * 8 + (P(None, "dp"),) * 4
    return jax.shard_map(
        functools.partial(per_device, mesh.shape["dp"], mesh.shape["rep"]),
        mesh=mesh,
        in_specs=(rows,) * 7 + owned,
        out_specs=(rows,) * 3 + made + (P(),),
        check_vma=False,
    )
```
